32 devices in a mesh: tm: 4 (over y, x), rows: 8 (over z, core).
Axes of the slice: x: 2, y: 2, z: 4, core: 2. Of those that a mesh axis runs over, the one named last changes fastest.
Arguments:
- queries: bfloat16 [16, 64, 16, 1792], P('tm', 'rows'), may hold values from -60 to 60
- keys: bfloat16 [16, 64, 16, 1792], P('tm', 'rows'), may hold values from -6 to 6
- values: bfloat16 [16, 64, 16, 1792], P('tm', 'rows'), may hold values from -6 to 6
- out_grad: bfloat16 [16, 64, 16, 1792], P('tm', 'rows'), may hold values from -6 to 6
Outputs:
- query_grad: bfloat16 [16, 64, 16, 1792], P('tm', 'rows')
- key_grad: bfloat16 [16, 64, 16, 1792], P('tm', 'rows')
- value_grad: bfloat16 [16, 64, 16, 1792], P('tm', 'rows')
The draws below stay inside these ranges and needn't reach their ends.
All inputs are finite; a program needn't handle non-finite values.
Results may differ from the reference program's by a relative error of at most 0.012.
Values may be sent and summed in bfloat16 or wider, within the bound.
No kernel may reach another device: no remote copies, remote signals or barrier semaphores. Data moves between devices by JAX's collectives and lax.ppermute only.
A program may use at most 128 MiB of HBM per device.

```python
import math
import jax
import jax.numpy as jnp
from jax import lax

WT = 4
WH = 8
WW = 8
HEADS = 14
HEAD_DIM = 128
COLS = 16
FRAMES = 16
ROWS = 64


def paired_fields(key):
    base = jax.random.fold_in(key, 17)
    key_query, key_key = jax.random.split(base, 2)
    shape = (FRAMES, ROWS, COLS, HEADS, HEAD_DIM)
    query_field = jnp.clip(jax.random.normal(key_query, shape, jnp.float32), -6.0, 6.0)
    key_field = jnp.clip(jax.random.normal(key_key, shape, jnp.float32), -6.0, 6.0)
    query_field = query_field.reshape(FRAMES, ROWS, COLS, HEADS * HEAD_DIM)
    key_field = key_field.reshape(FRAMES, ROWS, COLS, HEADS * HEAD_DIM)
    return (query_field, key_field)


def draw_queries(key, part):
    return paired_fields(key)[0].astype(jnp.bfloat16)


def draw_keys(key, part):
    return paired_fields(key)[1].astype(jnp.bfloat16)


def steps_of(key, dims, cuts, smallest, top_value):
    factor_of = 1.0
    for position, blocks in cuts:
        heights = jax.random.uniform(jax.random.fold_in(jax.random.fold_in(key, 6), position), (blocks,), jnp.float32, smallest / len(cuts), top_value / len(cuts))
        factor_of = factor_of * jnp.repeat(jnp.exp(heights), dims[position] // blocks).reshape((-1,) + (1,) * (len(dims) - 1 - position))
    return factor_of


def scatter_about(stream_key, extent, width, most, cuts=(), kind=jnp.bfloat16):
    values = jax.random.normal(stream_key, extent, jnp.float32) * width
    if len(cuts) > 0:
        values = steps_of(stream_key, extent, cuts, -0.22, 0.18) * values
    return jnp.clip(values, min=-most, max=most).astype(kind)


def setup_inputs(seed: int = 0) -> dict:
    key_of = jax.random.split(jax.random.key(seed), 5)
    return {
        "queries": draw_queries(jax.random.fold_in(key_of[4], 71), 0),
        "keys": draw_keys(jax.random.fold_in(key_of[4], 71), 0),
        "values": scatter_about(key_of[2], (FRAMES, ROWS, COLS, HEADS * HEAD_DIM), 1.0, 6.0, ((0, 4), (1, 8))),
        "out_grad": scatter_about(key_of[3], (FRAMES, ROWS, COLS, HEADS * HEAD_DIM), 1.0, 6.0, ((0, 4), (1, 8))),
    }


def window_grads(query_w, key_w, value_w, grad_w):
    factor = 1.0 / math.sqrt(query_w.shape[-1])
    query_f = query_w.astype(jnp.float32)
    key_f = key_w.astype(jnp.float32)
    value_f = value_w.astype(jnp.float32)
    grad_f = grad_w.astype(jnp.float32)
    scores = jnp.einsum('bhqd,bhkd->bhqk', query_f, key_f) * factor
    weights = jax.nn.softmax(scores, axis=-1)
    weights_b = weights.astype(jnp.bfloat16)
    weights_bf = weights_b.astype(jnp.float32)
    attended = jnp.einsum('bhqk,bhkd->bhqd', weights_bf, value_f)
    row_dot = lax.optimization_barrier(jnp.sum(grad_f * attended, axis=-1, keepdims=True))
    weight_grad = jnp.einsum('bhqd,bhkd->bhqk', grad_f, value_f)
    score_grad = (weights * (weight_grad - row_dot) * factor).astype(jnp.bfloat16).astype(jnp.float32)
    value_out = jnp.einsum('bhqk,bhqd->bhkd', weights_bf, grad_f).astype(jnp.bfloat16)
    query_out = jnp.einsum('bhqk,bhkd->bhqd', score_grad, key_f).astype(jnp.bfloat16)
    key_out = jnp.einsum('bhqk,bhqd->bhkd', score_grad, query_f).astype(jnp.bfloat16)
    return jnp.stack((query_out, key_out, value_out))

def reference(queries, keys, values, out_grad):
    total_frames, total_rows, columns, features = queries.shape
    slabs = total_frames // WT
    window_count = columns // WW
    row_windows = total_rows // WH
    length = WT * WH * WW

    def slab_grads(index):
        frame_ids = (index * WT + WT // 2 + jnp.arange(WT, dtype=jnp.int32)) % total_frames

        def prepare(field):
            piece = jnp.take(field, frame_ids, axis=0)
            piece = jnp.roll(piece, (-(WH // 2), -(WW // 2)), axis=(1, 2))
            piece = piece.reshape(WT, row_windows, WH, window_count, WW, HEADS, HEAD_DIM)
            return piece.transpose(1, 3, 5, 0, 2, 4, 6).reshape(row_windows, window_count, HEADS, length, HEAD_DIM)
        inputs = tuple((prepare(field) for field in (queries, keys, values, out_grad)))
        grads = lax.map(lambda group: window_grads(group[0], group[1], group[2], group[3]), inputs)
        grads = grads.reshape(row_windows, 3, window_count, HEADS, WT, WH, WW, HEAD_DIM)
        grads = grads.transpose(1, 4, 0, 5, 2, 6, 3, 7).reshape(3, WT, total_rows, columns, features)
        return jnp.roll(grads, (WH // 2, WW // 2), axis=(2, 3))
    stacked = lax.map(slab_grads, jnp.arange(slabs, dtype=jnp.int32))
    stacked = stacked.transpose(1, 0, 2, 3, 4, 5).reshape(3, total_frames, total_rows, columns, features)
    stacked = jnp.roll(stacked, WT // 2, axis=1)
    return (stacked[0], stacked[1], stacked[2])
```

```python
import math

import jax
import jax.numpy as jnp
from jax import lax
from jax.experimental import pallas as pl
from jax.experimental.pallas import tpu as pltpu
from jax.sharding import PartitionSpec as P

WW = 8
HEAD_DIM = 128
CHUNKS = 4
AXES = ("tm", "rows")
VMEM_BYTES = 40 * 1024 * 1024


def moved(value, by_time, by_rows):
    times, rows = lax.axis_size("tm"), lax.axis_size("rows")
    pairs = [
        (t * rows + r, ((t + by_time) % times) * rows + (r + by_rows) % rows)
        for t in range(times)
        for r in range(rows)
    ]
    return lax.ppermute(value, AXES, pairs)


def chunk_bounds(heads):
    count = min(CHUNKS, heads)
    sizes = [heads // count + (1 if i < heads % count else 0) for i in range(count)]
    bounds, start = [], 0
    for size in sizes:
        bounds.append((start, size))
        start += size
    return bounds


def late_half(shape):
    return lax.broadcasted_iota(jnp.int32, shape, 1) >= WW // 2


def split_windows(parts):
    tokens = jnp.concatenate(parts, axis=0).astype(jnp.float32)
    first, second = tokens[:, :WW], tokens[:, WW:]
    late = late_half(first.shape)
    flat = (first.shape[0] * WW, first.shape[2])
    inner = jnp.where(late, first, second).reshape(flat).astype(jnp.bfloat16)
    outer = jnp.where(late, second, first).reshape(flat).astype(jnp.bfloat16)
    return inner, outer


def join_windows(inner, outer):
    shape = (inner.shape[0] // WW, WW, inner.shape[1])
    inner, outer = inner.reshape(shape), outer.reshape(shape)
    late = late_half(shape)
    first = jnp.where(late, inner, outer)
    second = jnp.where(late, outer, inner)
    return jnp.concatenate((first, second), axis=1).astype(jnp.bfloat16)


def dot(a, b, dims):
    return lax.dot_general(a, b, (dims, ((), ())), preferred_element_type=jnp.float32)


def window_grads(query, key, value, grad):
    factor = 1.0 / math.sqrt(HEAD_DIM)
    scores = dot(key, query, ((1,), (1,))) * factor
    top = jnp.max(scores, axis=0, keepdims=True)
    weights = jnp.exp(scores - top)
    weights = weights * (1.0 / jnp.sum(weights, axis=0, keepdims=True))
    weights_b = weights.astype(jnp.bfloat16)
    weight_grad = dot(value, grad, ((1,), (1,)))
    row_dot = jnp.sum(weights_b.astype(jnp.float32) * weight_grad, axis=0, keepdims=True)
    score_grad = (weights * (weight_grad - row_dot) * factor).astype(jnp.bfloat16)
    value_out = dot(weights_b, grad, ((1,), (0,)))
    key_out = dot(score_grad, query, ((1,), (0,)))
    query_out = dot(score_grad, key, ((0,), (0,)))
    return query_out, key_out, value_out


def grads_kernel(*refs):
    q_ref, k_ref, v_ref, g_ref, row_ref, time_ref, corner_ref = refs[:7]
    frames, rows, columns, depth = q_ref.shape
    slots = frames * rows
    windows = []
    for index, ref in enumerate((q_ref, k_ref, v_ref, g_ref)):
        parts = [ref[...], row_ref[index], time_ref[index], corner_ref[index]]
        windows.append(split_windows([p.reshape(slots, columns, depth) for p in parts]))
    inner = window_grads(*[w[0] for w in windows])
    outer = window_grads(*[w[1] for w in windows])
    for index in range(3):
        tokens = join_windows(inner[index], outer[index])
        tokens = tokens.reshape(4, frames, rows, columns, depth)
        for place, ref in enumerate(refs[7:]):
            ref[index] = tokens[place]


def chunk_grads(inputs, received, start, size):
    frames, rows, columns, features = inputs[0].shape
    half = (frames // 2, rows // 2, columns)
    own = pl.BlockSpec(half + (HEAD_DIM,), lambda h: (1, 1, 0, start + h))
    sent = lambda n: pl.BlockSpec((n,) + half + (HEAD_DIM,), lambda h: (0, 0, 0, 0, h))
    piece = jax.ShapeDtypeStruct((3,) + half + (size * HEAD_DIM,), jnp.bfloat16)
    length = 4 * half[0] * half[1] * WW
    return pl.pallas_call(
        grads_kernel,
        grid=(size,),
        in_specs=[own] * 4 + [sent(4)] * 3,
        out_specs=[sent(3)] * 4,
        out_shape=[piece] * 4,
        compiler_params=pltpu.CompilerParams(vmem_limit_bytes=VMEM_BYTES),
        cost_estimate=pl.CostEstimate(
            flops=size * 2 * 5 * 2 * length * length * HEAD_DIM,
            bytes_accessed=7 * 2 * size * 2 * length * HEAD_DIM,
            transcendentals=size * 2 * length * length,
        ),
    )(*inputs, *received)


def place_kernel(*refs):
    own_ref, row_ref, time_ref, corner_ref = refs[:4]
    for index, out in enumerate(refs[-3:]):
        frames, rows, _, _ = out.shape
        f, r = frames // 2, rows // 2
        out[f:, r:] = own_ref[index]
        out[f:, :r] = row_ref[index]
        out[:f, r:] = time_ref[index]
        out[:f, :r] = corner_ref[index]


def placed(outs, pieces, whole, start, size):
    frames, rows, columns, features = whole.shape
    half = (frames // 2, rows // 2, columns)
    sent = pl.BlockSpec((3,) + half + (HEAD_DIM,), lambda h: (0, 0, 0, 0, h))
    full = pl.BlockSpec((frames, rows, columns, HEAD_DIM), lambda h: (0, 0, 0, start + h))
    outs = () if outs is None else outs
    return pl.pallas_call(
        place_kernel,
        grid=(size,),
        in_specs=[sent] * 4 + [pl.BlockSpec(memory_space=pl.ANY)] * len(outs),
        out_specs=[full] * 3,
        out_shape=[jax.ShapeDtypeStruct(whole.shape, whole.dtype)] * 3,
        input_output_aliases={4 + i: i for i in range(len(outs))},
        compiler_params=pltpu.CompilerParams(vmem_limit_bytes=VMEM_BYTES),
        cost_estimate=pl.CostEstimate(
            flops=0, bytes_accessed=sum(4 * p.size for p in pieces), transcendentals=0
        ),
    )(*pieces, *outs)


def shards(queries, keys, values, out_grad):
    inputs = (queries, keys, values, out_grad)
    frames, rows, columns, features = queries.shape
    early_f, late_f = slice(0, frames // 2), slice(frames // 2, frames)
    early_r, late_r = slice(0, rows // 2), slice(rows // 2, rows)
    bounds = chunk_bounds(features // HEAD_DIM)
    received = []
    for start, size in bounds:
        lanes = slice(start * HEAD_DIM, (start + size) * HEAD_DIM)
        cut = lambda f, r: jnp.stack([x[f, r, :, lanes] for x in inputs])
        time = moved(cut(early_f, late_r), -1, 0)
        corner = moved(cut(early_f, early_r), -1, -1)
        row = moved(cut(late_f, early_r), 0, -1)
        received.append((row, time, corner))
    returned = []
    for (start, size), got in zip(bounds, received):
        own, row, time, corner = chunk_grads(inputs, got, start, size)
        time = moved(time, 1, 0)
        corner = moved(corner, 1, 1)
        row = moved(row, 0, 1)
        returned.append((own, row, time, corner))
    outs = None
    for (start, size), pieces in zip(bounds, returned):
        outs = placed(outs, pieces, queries, start, size)
    return tuple(outs)


def solution(mesh):
    spec = P("tm", "rows", None, None)
    return jax.shard_map(
        shards,
        mesh=mesh,
        in_specs=(spec,) * 4,
        out_specs=(spec,) * 3,
        check_vma=False,
    )
```

```python
import math

import jax
import jax.numpy as jnp
from jax import lax
from jax.experimental import pallas as pl
from jax.experimental.pallas import tpu as pltpu
from jax.sharding import PartitionSpec as P

WW = 8
HEAD_DIM = 128
AXES = ("tm", "rows")
VMEM_BYTES = 40 * 1024 * 1024


def moved(value, parity, by_rows):
    times, rows = lax.axis_size("tm"), lax.axis_size("rows")
    pairs = []
    for t in range(times):
        step = 0 if parity is None else (1 if t % 2 == parity else -1)
        for r in range(rows):
            pairs.append((t * rows + r, ((t + step) % times) * rows + (r + by_rows) % rows))
    return lax.ppermute(value, AXES, pairs)


def late_half(shape):
    return lax.broadcasted_iota(jnp.int32, shape, 1) >= WW // 2


def split_windows(parts):
    tokens = jnp.concatenate(parts, axis=0).astype(jnp.float32)
    first, second = tokens[:, :WW], tokens[:, WW:]
    late = late_half(first.shape)
    flat = (first.shape[0] * WW, first.shape[2])
    inner = jnp.where(late, first, second).reshape(flat).astype(jnp.bfloat16)
    outer = jnp.where(late, second, first).reshape(flat).astype(jnp.bfloat16)
    return inner, outer


def join_windows(inner, outer):
    shape = (inner.shape[0] // WW, WW, inner.shape[1])
    inner, outer = inner.reshape(shape), outer.reshape(shape)
    late = late_half(shape)
    first = jnp.where(late, inner, outer)
    second = jnp.where(late, outer, inner)
    return jnp.concatenate((first, second), axis=1).astype(jnp.bfloat16)


def dot(a, b, dims):
    return lax.dot_general(a, b, (dims, ((), ())), preferred_element_type=jnp.float32)


def key_sum(value):
    return jnp.sum(value, axis=0, keepdims=True)


def products(query, key, value, grad):
    factor = 1.0 / math.sqrt(HEAD_DIM)
    scores = dot(key, query, ((1,), (1,))) * factor
    weight_grad = dot(value, grad, ((1,), (1,)))
    return scores, weight_grad


def partial_stats(query, key, value, grad):
    scores, weight_grad = products(query, key, value, grad)
    top = jnp.max(scores, axis=0, keepdims=True)
    powers = jnp.exp(scores - top)
    return top, key_sum(powers), key_sum(powers * weight_grad)


def partial_grads(query, key, value, grad, mine, other):
    factor = 1.0 / math.sqrt(HEAD_DIM)
    top = jnp.maximum(mine[0], other[0])
    scale_mine, scale_other = jnp.exp(mine[0] - top), jnp.exp(other[0] - top)
    inverse = 1.0 / (mine[1] * scale_mine + other[1] * scale_other)
    row_dot = (mine[2] * scale_mine + other[2] * scale_other) * inverse
    scores, weight_grad = products(query, key, value, grad)
    weights = jnp.exp(scores - top) * inverse
    score_grad = (weights * (weight_grad - row_dot) * factor).astype(jnp.bfloat16)
    value_out = dot(weights.astype(jnp.bfloat16), grad, ((1,), (0,)))
    key_out = dot(score_grad, query, ((1,), (0,)))
    query_out = dot(score_grad, key, ((0,), (0,)))
    return query_out, key_out, value_out


def window_tokens(refs, head):
    q_ref, k_ref, v_ref, g_ref, qg_ref, key_row_ref, value_row_ref, near_ref, corner_ref = refs
    frames, rows, columns, _ = q_ref.shape
    lanes = pl.ds(head * HEAD_DIM, HEAD_DIM)
    flat = lambda p: p.reshape(frames * rows, columns, HEAD_DIM)
    at = lambda ref, *index: flat(ref[(*index, slice(None), slice(None), slice(None), lanes)])
    query = split_windows([at(q_ref), at(qg_ref, 0)])
    grad = split_windows([at(g_ref), at(qg_ref, 1)])
    key = split_windows([at(k_ref), at(key_row_ref, 0)])
    value = split_windows([at(v_ref), at(value_row_ref, 0)])
    far_query = split_windows([at(near_ref, 0), at(corner_ref, 0)])
    far_grad = split_windows([at(near_ref, 1), at(corner_ref, 1)])
    both = lambda own, far: jnp.concatenate((own, far), axis=0)
    return [
        (both(query[w], far_query[w]), key[w], value[w], both(grad[w], far_grad[w])) for w in (0, 1)
    ]


def stats_kernel(late_ref, *refs):
    out = refs[9]
    for head in range(out.shape[0]):
        found = []
        for window in window_tokens(refs[:9], head):
            found.extend(partial_stats(*window))
        blank = jnp.zeros_like(found[0])
        out[head] = jnp.concatenate(found + [blank] * (out.shape[1] - len(found)), axis=0)


def grads_kernel(late_ref, *refs):
    mine_ref, other_ref, kept_out = refs[9:12]
    if len(refs) == 14:
        row_outs = [refs[12].at[index] for index in range(3)]
        near_out, corner_out = refs[13].at[0], refs[13].at[1]
    else:
        row_outs = [refs[12], refs[13].at[0], refs[13].at[1]]
        near_out, corner_out = refs[14:]
    _, frames, rows, columns, width = kept_out.shape
    shape = (2, frames, rows, columns, HEAD_DIM)
    for head in range(width // HEAD_DIM):
        lanes = pl.ds(head * HEAD_DIM, HEAD_DIM)
        grads = []
        for w, window in enumerate(window_tokens(refs[:9], head)):
            mine = [mine_ref[head, pl.ds(3 * w + i, 1)] for i in range(3)]
            other = [other_ref[head, pl.ds(3 * w + i, 1)] for i in range(3)]
            half = window[1].shape[0]
            other = [jnp.concatenate((o[:, half:], o[:, :half]), axis=1) for o in other]
            grads.append(partial_grads(*window, mine, other))
        kept = [[g[0][:half] for g in grads], [g[1] for g in grads], [g[2] for g in grads]]
        for index, windows in enumerate(kept):
            tokens = join_windows(*windows).reshape(shape)
            kept_out[index, :, :, :, lanes] = tokens[0]
            row_outs[index][:, :, :, lanes] = tokens[1]
        tokens = join_windows(*[g[0][half:] for g in grads]).reshape(shape)
        near_out[:, :, :, lanes] = tokens[0]
        corner_out[:, :, :, lanes] = tokens[1]


def lane_block(shape, lanes, place=None):
    index = lambda h, late: ((0,) * (len(shape) - 1) if place is None else place(late)) + (h,)
    return pl.BlockSpec(tuple(shape[:-1]) + (lanes,), index)


def heads_per_step(heads):
    return 2 if heads % 2 == 0 else 1


def small():
    return pl.CostEstimate(flops=1, bytes_accessed=1, transcendentals=0)


def called(kernel, late, operands, in_specs, out_specs, out_shape, steps, aliases=None):
    return pl.pallas_call(
        kernel,
        grid_spec=pltpu.PrefetchScalarGridSpec(
            num_scalar_prefetch=1, grid=(steps,), in_specs=in_specs, out_specs=out_specs
        ),
        out_shape=out_shape,
        input_output_aliases=aliases or {},
        compiler_params=pltpu.CompilerParams(vmem_limit_bytes=VMEM_BYTES),
        cost_estimate=small(),
    )(late, *operands)


def window_specs(inputs, received, lanes):
    frames, rows, columns, _ = inputs[0].shape
    own = lane_block((frames // 2, rows // 2, columns, 0), lanes, lambda late: (late[0], 1, 0))
    return [own] * 4 + [lane_block(r.shape, lanes) for r in received]


def stats_block(heads, length):
    return pl.BlockSpec((heads, 8, length), lambda h, late: (h, 0, 0))


def family_stats(late, inputs, received):
    frames, rows, _, features = inputs[0].shape
    heads, length = features // HEAD_DIM, frames * rows * WW
    step = heads_per_step(heads)
    return called(
        stats_kernel,
        late,
        (*inputs, *received),
        window_specs(inputs, received, step * HEAD_DIM),
        stats_block(step, length),
        jax.ShapeDtypeStruct((heads, 8, length), jnp.float32),
        heads // step,
    )


def family_grads(late, inputs, received, mine, other, joined):
    frames, rows, columns, features = inputs[0].shape
    heads, length = features // HEAD_DIM, frames * rows * WW
    step = heads_per_step(heads)
    sent = jax.ShapeDtypeStruct((frames // 2, rows // 2, columns, features), jnp.bfloat16)
    kept = jax.ShapeDtypeStruct((3,) + sent.shape, jnp.bfloat16)
    two = jax.ShapeDtypeStruct((2,) + sent.shape, jnp.bfloat16)
    shapes = [kept, kept, two] if joined else [kept, sent, two, sent, sent]
    return called(
        grads_kernel,
        late,
        (*inputs, *received, mine, other),
        window_specs(inputs, received, step * HEAD_DIM) + [stats_block(step, length)] * 2,
        [lane_block(s.shape, step * HEAD_DIM) for s in shapes],
        shapes,
        heads // step,
    )


def place_pair_kernel(late_ref, *refs):
    own_ref, outs = refs[0], refs[-2:]
    row_ref = refs[1]
    first = row_ref.shape[0] - len(outs)
    for index, out in enumerate(outs):
        half = out.shape[1] // 2
        out[:, half:] = own_ref[1 + index]
        out[:, :half] = row_ref[first + index]


def place_sum_kernel(late_ref, *refs):
    own_ref, row_ref, near_ref, corner_ref = refs[:4]
    out = refs[-1]
    half = out.shape[1] // 2
    row_ref, near_ref = [r if r.ndim == 4 else r.at[0] for r in (row_ref, near_ref)]
    total = lambda a, b: (a.astype(jnp.float32) + b.astype(jnp.float32)).astype(jnp.bfloat16)
    out[:, half:] = total(own_ref[0], near_ref[...])
    out[:, :half] = total(row_ref[...], corner_ref[...])


def placed(kernel, number, late, outs, pieces, counts, whole):
    frames, rows, columns, features = whole.shape
    lanes = features // heads_per_step(features // HEAD_DIM)
    outs = () if outs is None else outs
    shape = lambda p, n: ((n,) + p.shape[1:]) if p.ndim == 5 else p.shape
    full = lane_block((frames // 2, rows, columns, 0), lanes, lambda late: (late[0], 0, 0))
    return called(
        kernel,
        late,
        (*pieces, *outs),
        [lane_block(shape(p, n), lanes) for p, n in zip(pieces, counts)]
        + [pl.BlockSpec(memory_space=pl.ANY)] * len(outs),
        [full] * number,
        [jax.ShapeDtypeStruct(whole.shape, whole.dtype)] * number,
        features // lanes,
        {1 + len(pieces) + i: i for i in range(len(outs))},
    )


def after(value, *earlier):
    return lax.optimization_barrier((value,) + earlier)[0]


def shards(queries, keys, values, out_grad):
    inputs = (queries, keys, values, out_grad)
    frames, rows, columns, features = queries.shape
    time = lax.axis_index("tm")
    late = [jnp.where(time % 2 == parity, 1, 0).astype(jnp.int32) for parity in (0, 1)]

    def cut(xs, parity, row_start):
        sizes = (frames // 2, rows // 2, columns, features)
        start = (late[parity] * (frames // 2), row_start, 0, 0)
        return jnp.stack([lax.dynamic_slice(x, start, sizes) for x in xs])

    def near_of(parity, *wait):
        return moved(after(cut((queries, out_grad), parity, rows // 2), *wait), parity, 0)

    def row_of(xs, parity, *wait):
        return moved(after(cut(xs, parity, 0), *wait), None, -1)

    def rows_of_both(parity, *wait):
        return [row_of((x,), parity, *wait) for x in (keys, values)]

    qg = (queries, out_grad)
    spot = [flag.reshape(1) for flag in late]
    near0 = near_of(0)
    row_qg0 = row_of(qg, 0)
    corner0 = moved(row_qg0, 0, 0)
    row_kv0 = rows_of_both(0, row_qg0)
    near1 = near_of(1, near0)
    got0 = (row_qg0, *row_kv0, near0, corner0)
    stats0 = family_stats(spot[0], inputs, got0)
    other0 = moved(stats0, 0, 0)
    row_qg1 = jnp.concatenate([row_of((x,), 1, *row_kv0) for x in qg])
    row_kv1 = rows_of_both(1, other0)
    corner1 = moved(after(row_qg1, other0, near1), 1, 0)
    kept0, row0, far0 = family_grads(spot[0], inputs, got0, stats0, other0, True)
    got1 = (row_qg1, *row_kv1, near1, after(corner1, far0))
    stats1 = family_stats(spot[1], inputs, got1)
    other1 = moved(stats1, 1, 0)
    row0 = moved(after(row0, *row_kv1), None, 1)
    far0 = moved(after(far0, other1), 0, 0)
    kept1, row1, pair1, near_b1, corner_b1 = family_grads(
        spot[1], inputs, got1, stats1, after(other1, row0), False
    )
    near_b1 = moved(after(near_b1, far0), 1, 0)
    corner_b1 = moved(corner_b1, 1, 1)
    row1, pair1 = moved(row1, None, 1), moved(pair1, None, 1)
    corner_b0 = moved(after(far0[1], row1), None, 1)
    pair = placed(place_pair_kernel, 2, spot[0], None, (kept0, row0), (3, 3), queries)
    total = placed(
        place_sum_kernel, 1, spot[0], None, (kept0, row0, far0, corner_b0), (1, 1, 1, 1), queries
    )
    pair = placed(place_pair_kernel, 2, spot[1], pair, (kept1, pair1), (3, 2), queries)
    total = placed(
        place_sum_kernel, 1, spot[1], total, (kept1, row1, near_b1, corner_b1), (1, 1, 1, 1), queries
    )
    return (total[0], pair[0], pair[1])


def solution(mesh):
    spec = P("tm", "rows", None, None)
    return jax.shard_map(
        shards,
        mesh=mesh,
        in_specs=(spec,) * 4,
        out_specs=(spec,) * 3,
        check_vma=False,
    )
```

```python
import math

import jax
import jax.numpy as jnp
from jax import lax
from jax.experimental import pallas as pl
from jax.experimental.pallas import tpu as pltpu
from jax.sharding import PartitionSpec as P

WW = 8
HEAD_DIM = 128
AXES = ("tm", "rows")
VMEM_BYTES = 40 * 1024 * 1024


def moved(value, parity, by_rows):
    times, rows = lax.axis_size("tm"), lax.axis_size("rows")
    pairs = []
    for t in range(times):
        step = 0 if parity is None else (1 if t % 2 == parity else -1)
        for r in range(rows):
            pairs.append((t * rows + r, ((t + step) % times) * rows + (r + by_rows) % rows))
    return lax.ppermute(value, AXES, pairs)


def middle(shape):
    column = lax.broadcasted_iota(jnp.int32, shape, 1)
    return (column >= WW // 2) & (column < WW + WW // 2)


def turned(tokens):
    return jnp.concatenate((tokens[:, WW:], tokens[:, :WW]), axis=1)


def split_windows(parts):
    first, second = parts[0], turned(parts[1])
    inside = middle(first.shape)
    flat = (first.shape[0] * first.shape[1], first.shape[2])
    inner = jnp.where(inside, first, second).reshape(flat)
    outer = jnp.where(inside, second, first).reshape(flat)
    return inner, outer


def join_windows(inner, outer, slots):
    shape = (slots, 2 * WW, inner.shape[1])
    inner = inner.astype(jnp.bfloat16).reshape(shape)
    outer = outer.astype(jnp.bfloat16).reshape(shape)
    inside = middle(shape)
    return jnp.where(inside, inner, outer), turned(jnp.where(inside, outer, inner))


def dot(a, b, dims):
    return lax.dot_general(a, b, (dims, ((), ())), preferred_element_type=jnp.float32)


def key_sum(value):
    return jnp.sum(value, axis=0, keepdims=True)


def products(query, key, value, grad):
    factor = 1.0 / math.sqrt(HEAD_DIM)
    scores = dot(key, query, ((1,), (1,))) * factor
    weight_grad = dot(value, grad, ((1,), (1,)))
    return scores, weight_grad


def partial_stats(query, key, value, grad):
    scores, weight_grad = products(query, key, value, grad)
    top = jnp.max(scores, axis=0, keepdims=True)
    powers = jnp.exp(scores - top)
    return top, key_sum(powers), key_sum(powers * weight_grad)


def partial_grads(windows, mine, other):
    factor = 1.0 / math.sqrt(HEAD_DIM)
    each = range(len(windows))
    made = [products(*w) for w in windows]
    tops, inverses, row_dots = [], [], []
    for a, b in zip(mine, other):
        top = jnp.maximum(a[0], b[0])
        scale_a, scale_b = jnp.exp(a[0] - top), jnp.exp(b[0] - top)
        inverse = 1.0 / (a[1] * scale_a + b[1] * scale_b)
        tops.append(top)
        inverses.append(inverse)
        row_dots.append((a[2] * scale_a + b[2] * scale_b) * inverse)
    weights = [jnp.exp(made[i][0] - tops[i]) * inverses[i] for i in each]
    weights_b = [w.astype(jnp.bfloat16) for w in weights]
    score_grads = [
        (weights[i] * ((made[i][1] - row_dots[i]) * factor)).astype(jnp.bfloat16) for i in each
    ]
    value_out = [dot(weights_b[i], windows[i][3], ((1,), (0,))) for i in each]
    key_out = [dot(score_grads[i], windows[i][0], ((1,), (0,))) for i in each]
    query_out = [dot(score_grads[i], windows[i][1], ((0,), (0,))) for i in each]
    return list(zip(query_out, key_out, value_out))


def window_tokens(refs, head):
    q_ref, k_ref, v_ref, g_ref, qg_ref, key_row_ref, value_row_ref, near_ref, corner_ref = refs
    frames, rows, columns, _ = q_ref.shape
    lanes = pl.ds(head * HEAD_DIM, HEAD_DIM)
    flat = lambda p: p.reshape(frames * rows, columns, HEAD_DIM)
    at = lambda ref, *index: flat(ref[(*index, slice(None), slice(None), slice(None), lanes)])
    query = split_windows([at(q_ref), at(qg_ref, 0)])
    grad = split_windows([at(g_ref), at(qg_ref, 1)])
    key = split_windows([at(k_ref), at(key_row_ref, 0)])
    value = split_windows([at(v_ref), at(value_row_ref, 0)])
    far_query = split_windows([at(near_ref, 0), at(corner_ref, 0)])
    far_grad = split_windows([at(near_ref, 1), at(corner_ref, 1)])
    both = lambda own, far: jnp.concatenate((own, far), axis=0)
    return [
        (both(query[w], far_query[w]), key[w], value[w], both(grad[w], far_grad[w])) for w in (0, 1)
    ]


def stats_kernel(late_ref, *refs):
    out = refs[9]
    for head in range(out.shape[0]):
        found = []
        for window in window_tokens(refs[:9], head):
            found.extend(partial_stats(*window))
        blank = jnp.zeros_like(found[0])
        out[head] = jnp.concatenate(found + [blank] * (out.shape[1] - len(found)), axis=0)


def grads_kernel(late_ref, *refs):
    mine_ref, other_ref, kept_out = refs[9:12]
    near_out, corner_out = refs[-2:]
    row_outs = [refs[12], refs[13].at[0], refs[13].at[1]]
    _, frames, rows, columns, width = kept_out.shape
    shape = (frames, rows, columns, HEAD_DIM)
    for head in range(width // HEAD_DIM):
        lanes = pl.ds(head * HEAD_DIM, HEAD_DIM)
        windows = window_tokens(refs[:9], head)
        half = windows[0][1].shape[0]
        stat = lambda ref, w: [ref[head, pl.ds(3 * w + i, 1)] for i in range(3)]
        swapped = lambda o: jnp.concatenate((o[:, half:], o[:, :half]), axis=1)
        mine = [stat(mine_ref, w) for w in (0, 1)]
        other = [[swapped(o) for o in stat(other_ref, w)] for w in (0, 1)]
        grads = partial_grads(windows, mine, other)
        kept = [[g[0][:half] for g in grads], [g[1] for g in grads], [g[2] for g in grads]]
        for index, windows in enumerate(kept):
            tokens = [p.reshape(shape) for p in join_windows(*windows, frames * rows)]
            kept_out[index, :, :, :, lanes] = tokens[0]
            row_outs[index][:, :, :, lanes] = tokens[1]
        tokens = [p.reshape(shape) for p in join_windows(*[g[0][half:] for g in grads], frames * rows)]
        near_out[:, :, :, lanes] = tokens[0]
        corner_out[:, :, :, lanes] = tokens[1]


def lane_block(shape, lanes, place=None):
    index = lambda h, late: ((0,) * (len(shape) - 1) if place is None else place(late)) + (h,)
    return pl.BlockSpec(tuple(shape[:-1]) + (lanes,), index)


def heads_per_step(heads):
    return next(n for n in range(14, 0, -1) if heads % n == 0)


def small():
    return pl.CostEstimate(flops=1, bytes_accessed=1, transcendentals=0)


def called(kernel, late, operands, in_specs, out_specs, out_shape, steps, aliases=None):
    return pl.pallas_call(
        kernel,
        grid_spec=pltpu.PrefetchScalarGridSpec(
            num_scalar_prefetch=1, grid=(steps,), in_specs=in_specs, out_specs=out_specs
        ),
        out_shape=out_shape,
        input_output_aliases=aliases or {},
        compiler_params=pltpu.CompilerParams(vmem_limit_bytes=VMEM_BYTES),
        cost_estimate=small(),
    )(late, *operands)


def window_specs(inputs, received, lanes):
    frames, rows, columns, _ = inputs[0].shape
    own = lane_block((frames // 2, rows // 2, columns, 0), lanes, lambda late: (late[0], 1, 0))
    return [own] * 4 + [lane_block(r.shape, lanes) for r in received]


def stats_block(heads, length):
    return pl.BlockSpec((heads, 8, length), lambda h, late: (h, 0, 0))


def family_stats(late, inputs, received):
    frames, rows, _, features = inputs[0].shape
    heads, length = features // HEAD_DIM, frames * rows * WW
    step = heads_per_step(heads)
    return called(
        stats_kernel,
        late,
        (*inputs, *received),
        window_specs(inputs, received, step * HEAD_DIM),
        stats_block(step, length),
        jax.ShapeDtypeStruct((heads, 8, length), jnp.float32),
        heads // step,
    )


def family_grads(late, inputs, received, mine, other):
    frames, rows, columns, features = inputs[0].shape
    heads, length = features // HEAD_DIM, frames * rows * WW
    step = heads_per_step(heads)
    sent = jax.ShapeDtypeStruct((frames // 2, rows // 2, columns, features), jnp.bfloat16)
    kept = jax.ShapeDtypeStruct((3,) + sent.shape, jnp.bfloat16)
    two = jax.ShapeDtypeStruct((2,) + sent.shape, jnp.bfloat16)
    shapes = [kept, sent, two, sent, sent]
    return called(
        grads_kernel,
        late,
        (*inputs, *received, mine, other),
        window_specs(inputs, received, step * HEAD_DIM) + [stats_block(step, length)] * 2,
        [lane_block(s.shape, step * HEAD_DIM) for s in shapes],
        shapes,
        heads // step,
    )


def place_pair_kernel(late_ref, *refs):
    own_ref, outs = refs[0], refs[-2:]
    row_ref = refs[1]
    first = row_ref.shape[0] - len(outs)
    for index, out in enumerate(outs):
        half = out.shape[1] // 2
        out[:, half:] = own_ref[1 + index]
        out[:, :half] = row_ref[first + index]


def place_sum_kernel(late_ref, *refs):
    own_ref, row_ref, near_ref, corner_ref = refs[:4]
    out = refs[-1]
    half = out.shape[1] // 2
    row_ref, near_ref = [r if r.ndim == 4 else r.at[0] for r in (row_ref, near_ref)]
    total = lambda a, b: (a.astype(jnp.float32) + b.astype(jnp.float32)).astype(jnp.bfloat16)
    out[:, half:] = total(own_ref[0], near_ref[...])
    out[:, :half] = total(row_ref[...], corner_ref[...])


def placed(kernel, number, late, outs, pieces, counts, whole):
    frames, rows, columns, features = whole.shape
    lanes = features // 2
    outs = () if outs is None else outs
    shape = lambda p, n: ((n,) + p.shape[1:]) if p.ndim == 5 else p.shape
    full = lane_block((frames // 2, rows, columns, 0), lanes, lambda late: (late[0], 0, 0))
    return called(
        kernel,
        late,
        (*pieces, *outs),
        [lane_block(shape(p, n), lanes) for p, n in zip(pieces, counts)]
        + [pl.BlockSpec(memory_space=pl.ANY)] * len(outs),
        [full] * number,
        [jax.ShapeDtypeStruct(whole.shape, whole.dtype)] * number,
        features // lanes,
        {1 + len(pieces) + i: i for i in range(len(outs))},
    )


def after(value, *earlier):
    return lax.optimization_barrier((value,) + earlier)[0]


def shards(queries, keys, values, out_grad):
    inputs = (queries, keys, values, out_grad)
    frames, rows, columns, features = queries.shape
    time = lax.axis_index("tm")
    late = [jnp.where(time % 2 == parity, 1, 0).astype(jnp.int32) for parity in (0, 1)]

    def cut(xs, parity, row_start):
        sizes = (frames // 2, rows // 2, columns, features)
        start = (late[parity] * (frames // 2), row_start, 0, 0)
        return jnp.stack([lax.dynamic_slice(x, start, sizes) for x in xs])

    def near_of(parity, *wait):
        return moved(after(cut((queries, out_grad), parity, rows // 2), *wait), parity, 0)

    def row_of(xs, parity, *wait):
        return moved(after(cut(xs, parity, 0), *wait), None, -1)

    def rows_of_both(parity, *wait):
        return [row_of((x,), parity, *wait) for x in (keys, values)]

    qg = (queries, out_grad)
    spot = [flag.reshape(1) for flag in late]
    near0 = near_of(0)
    row_qg0 = row_of(qg, 0)
    corner0 = moved(row_qg0, 0, 0)
    row_kv0 = rows_of_both(0, row_qg0)
    near1 = near_of(1, near0)
    got0 = (row_qg0, *row_kv0, near0, corner0)
    stats0 = family_stats(spot[0], inputs, got0)
    other0 = moved(stats0, 0, 0)
    row_qg1 = jnp.concatenate([row_of((x,), 1, *row_kv0) for x in qg])
    row_kv1 = rows_of_both(1, other0)
    corner1 = moved(after(row_qg1, other0, near1), 1, 0)
    kept0, row0, pair0, near_b0, corner_b0 = family_grads(spot[0], inputs, got0, stats0, other0)
    got1 = (row_qg1, *row_kv1, near1, after(corner1, corner_b0))
    stats1 = family_stats(spot[1], inputs, got1)
    other1 = moved(stats1, 1, 0)
    row0, pair0 = [moved(after(r, *row_kv1), None, 1) for r in (row0, pair0)]
    near_b0 = moved(near_b0, 0, 0)
    corner_b0 = moved(after(corner_b0, other1), 0, 1)
    kept1, row1, pair1, near_b1, corner_b1 = family_grads(
        spot[1], inputs, got1, stats1, after(other1, row0, pair0, near_b0)
    )
    near_b1 = moved(near_b1, 1, 0)
    corner_b1 = moved(after(corner_b1, near_b0, corner_b0), 1, 1)
    row1, pair1 = moved(row1, None, 1), moved(pair1, None, 1)
    pair = placed(place_pair_kernel, 2, spot[0], None, (kept0, pair0), (3, 2), queries)
    total = placed(
        place_sum_kernel, 1, spot[0], None, (kept0, row0, near_b0, corner_b0), (1, 1, 1, 1), queries
    )
    pair = placed(place_pair_kernel, 2, spot[1], pair, (kept1, pair1), (3, 2), queries)
    total = placed(
        place_sum_kernel, 1, spot[1], total, (kept1, row1, near_b1, corner_b1), (1, 1, 1, 1), queries
    )
    return (total[0], pair[0], pair[1])


def solution(mesh):
    spec = P("tm", "rows", None, None)
    return jax.shard_map(
        shards,
        mesh=mesh,
        in_specs=(spec,) * 4,
        out_specs=(spec,) * 3,
        check_vma=False,
    )
```

```python
import math

import jax
import jax.numpy as jnp
from jax import lax
from jax.experimental import pallas as pl
from jax.experimental.pallas import tpu as pltpu
from jax.sharding import PartitionSpec as P

WW = 8
HEAD_DIM = 128
AXES = ("tm", "rows")
VMEM_BYTES = 40 * 1024 * 1024


def moved(value, parity, by_rows):
    times, rows = lax.axis_size("tm"), lax.axis_size("rows")
    pairs = []
    for t in range(times):
        step = 0 if parity is None else (1 if t % 2 == parity else -1)
        for r in range(rows):
            pairs.append((t * rows + r, ((t + step) % times) * rows + (r + by_rows) % rows))
    return lax.ppermute(value, AXES, pairs)


def middle(shape):
    column = lax.broadcasted_iota(jnp.int32, shape, 1)
    return (column >= WW // 2) & (column < WW + WW // 2)


def turned(tokens):
    return jnp.concatenate((tokens[:, WW:], tokens[:, :WW]), axis=1)


def split_windows(parts):
    first, second = parts[0], turned(parts[1])
    inside = middle(first.shape)
    flat = (first.shape[0] * first.shape[1], first.shape[2])
    inner = jnp.where(inside, first, second).reshape(flat)
    outer = jnp.where(inside, second, first).reshape(flat)
    return inner, outer


def join_windows(inner, outer, slots):
    shape = (slots, 2 * WW, inner.shape[1])
    inner = inner.astype(jnp.bfloat16).reshape(shape)
    outer = outer.astype(jnp.bfloat16).reshape(shape)
    inside = middle(shape)
    return jnp.where(inside, inner, outer), turned(jnp.where(inside, outer, inner))


def dot(a, b, dims):
    return lax.dot_general(a, b, (dims, ((), ())), preferred_element_type=jnp.float32)


def key_sum(value):
    return jnp.sum(value, axis=0, keepdims=True)


def products(query, key, value, grad):
    factor = 1.0 / math.sqrt(HEAD_DIM)
    scores = dot(key, query, ((1,), (1,))) * factor
    weight_grad = dot(value, grad, ((1,), (1,)))
    return scores, weight_grad


def partial_stats(query, key, value, grad):
    scores, weight_grad = products(query, key, value, grad)
    top = jnp.max(scores, axis=0, keepdims=True)
    powers = jnp.exp(scores - top)
    return top, key_sum(powers), key_sum(powers * weight_grad)


def partial_grads(windows, mine, other):
    factor = 1.0 / math.sqrt(HEAD_DIM)
    each = range(len(windows))
    made = [products(*w) for w in windows]
    tops, inverses, row_dots = [], [], []
    for a, b in zip(mine, other):
        top = jnp.maximum(a[0], b[0])
        scale_a, scale_b = jnp.exp(a[0] - top), jnp.exp(b[0] - top)
        inverse = 1.0 / (a[1] * scale_a + b[1] * scale_b)
        tops.append(top)
        inverses.append(inverse)
        row_dots.append((a[2] * scale_a + b[2] * scale_b) * inverse)
    weights = [jnp.exp(made[i][0] - tops[i]) * inverses[i] for i in each]
    weights_b = [w.astype(jnp.bfloat16) for w in weights]
    score_grads = [
        (weights[i] * ((made[i][1] - row_dots[i]) * factor)).astype(jnp.bfloat16) for i in each
    ]
    value_out = [dot(weights_b[i], windows[i][3], ((1,), (0,))) for i in each]
    key_out = [dot(score_grads[i], windows[i][0], ((1,), (0,))) for i in each]
    query_out = [dot(score_grads[i], windows[i][1], ((0,), (0,))) for i in each]
    return list(zip(query_out, key_out, value_out))


def window_tokens(refs, head):
    q_ref, k_ref, v_ref, g_ref, qg_ref, key_row_ref, value_row_ref, near_ref, corner_ref = refs
    frames, rows, columns, _ = q_ref.shape
    lanes = pl.ds(head * HEAD_DIM, HEAD_DIM)
    flat = lambda p: p.reshape(frames * rows, columns, HEAD_DIM)
    at = lambda ref, *index: flat(ref[(*index, slice(None), slice(None), slice(None), lanes)])
    query = split_windows([at(q_ref), at(qg_ref, 0)])
    grad = split_windows([at(g_ref), at(qg_ref, 1)])
    key = split_windows([at(k_ref), at(key_row_ref, 0)])
    value = split_windows([at(v_ref), at(value_row_ref, 0)])
    far_query = split_windows([at(near_ref, 0), at(corner_ref, 0)])
    far_grad = split_windows([at(near_ref, 1), at(corner_ref, 1)])
    both = lambda own, far: jnp.concatenate((own, far), axis=0)
    return [
        (both(query[w], far_query[w]), key[w], value[w], both(grad[w], far_grad[w])) for w in (0, 1)
    ]


def stats_kernel(late_ref, *refs):
    out = refs[9]
    for head in range(out.shape[0]):
        found = []
        for window in window_tokens(refs[:9], head):
            found.extend(partial_stats(*window))
        blank = jnp.zeros_like(found[0])
        out[head] = jnp.concatenate(found + [blank] * (out.shape[1] - len(found)), axis=0)


def grads_kernel(late_ref, *refs):
    mine_ref, other_ref, kept_out = refs[9:12]
    near_out, corner_out = refs[-2:]
    row_outs = refs[12:15] if len(refs) == 17 else [refs[12], refs[13].at[0], refs[13].at[1]]
    _, frames, rows, columns, width = kept_out.shape
    shape = (frames, rows, columns, HEAD_DIM)
    for head in range(width // HEAD_DIM):
        lanes = pl.ds(head * HEAD_DIM, HEAD_DIM)
        windows = window_tokens(refs[:9], head)
        half = windows[0][1].shape[0]
        stat = lambda ref, w: [ref[head, pl.ds(3 * w + i, 1)] for i in range(3)]
        swapped = lambda o: jnp.concatenate((o[:, half:], o[:, :half]), axis=1)
        mine = [stat(mine_ref, w) for w in (0, 1)]
        other = [[swapped(o) for o in stat(other_ref, w)] for w in (0, 1)]
        grads = partial_grads(windows, mine, other)
        kept = [[g[0][:half] for g in grads], [g[1] for g in grads], [g[2] for g in grads]]
        for index, windows in enumerate(kept):
            tokens = [p.reshape(shape) for p in join_windows(*windows, frames * rows)]
            kept_out[index, :, :, :, lanes] = tokens[0]
            row_outs[index][:, :, :, lanes] = tokens[1]
        tokens = [p.reshape(shape) for p in join_windows(*[g[0][half:] for g in grads], frames * rows)]
        near_out[:, :, :, lanes] = tokens[0]
        corner_out[:, :, :, lanes] = tokens[1]


def lane_block(shape, lanes, place=None):
    index = lambda h, late: ((0,) * (len(shape) - 1) if place is None else place(late)) + (h,)
    return pl.BlockSpec(tuple(shape[:-1]) + (lanes,), index)


def heads_per_step(heads):
    return next(n for n in range(14, 0, -1) if heads % n == 0)


def small():
    return pl.CostEstimate(flops=1, bytes_accessed=1, transcendentals=0)


def called(kernel, late, operands, in_specs, out_specs, out_shape, steps, aliases=None):
    return pl.pallas_call(
        kernel,
        grid_spec=pltpu.PrefetchScalarGridSpec(
            num_scalar_prefetch=1, grid=(steps,), in_specs=in_specs, out_specs=out_specs
        ),
        out_shape=out_shape,
        input_output_aliases=aliases or {},
        compiler_params=pltpu.CompilerParams(vmem_limit_bytes=VMEM_BYTES),
        cost_estimate=small(),
    )(late, *operands)


def window_specs(inputs, received, lanes):
    frames, rows, columns, _ = inputs[0].shape
    own = lane_block((frames // 2, rows // 2, columns, 0), lanes, lambda late: (late[0], 1, 0))
    return [own] * 4 + [lane_block(r.shape, lanes) for r in received]


def stats_block(heads, length):
    return pl.BlockSpec((heads, 8, length), lambda h, late: (h, 0, 0))


def family_stats(late, inputs, received):
    frames, rows, _, features = inputs[0].shape
    heads, length = features // HEAD_DIM, frames * rows * WW
    step = heads_per_step(heads)
    return called(
        stats_kernel,
        late,
        (*inputs, *received),
        window_specs(inputs, received, step * HEAD_DIM),
        stats_block(step, length),
        jax.ShapeDtypeStruct((heads, 8, length), jnp.float32),
        heads // step,
    )


def family_grads(late, inputs, received, mine, other, joined):
    frames, rows, columns, features = inputs[0].shape
    heads, length = features // HEAD_DIM, frames * rows * WW
    step = heads_per_step(heads)
    sent = jax.ShapeDtypeStruct((frames // 2, rows // 2, columns, features), jnp.bfloat16)
    kept = jax.ShapeDtypeStruct((3,) + sent.shape, jnp.bfloat16)
    two = jax.ShapeDtypeStruct((2,) + sent.shape, jnp.bfloat16)
    shapes = [kept, sent] + ([two] if joined else [sent, sent]) + [sent, sent]
    return called(
        grads_kernel,
        late,
        (*inputs, *received, mine, other),
        window_specs(inputs, received, step * HEAD_DIM) + [stats_block(step, length)] * 2,
        [lane_block(s.shape, step * HEAD_DIM) for s in shapes],
        shapes,
        heads // step,
    )


def place_pair_kernel(late_ref, *refs):
    own_ref, outs = refs[0], refs[-2:]
    row_refs = refs[1:3] if refs[1].ndim == 4 else [refs[1].at[0], refs[1].at[1]]
    for index, out in enumerate(outs):
        half = out.shape[1] // 2
        out[:, half:] = own_ref[1 + index]
        out[:, :half] = row_refs[index][...]


def place_sum_kernel(late_ref, *refs):
    own_ref, row_ref, near_ref, corner_ref = refs[:4]
    out = refs[-1]
    half = out.shape[1] // 2
    row_ref, near_ref = [r if r.ndim == 4 else r.at[0] for r in (row_ref, near_ref)]
    total = lambda a, b: (a.astype(jnp.float32) + b.astype(jnp.float32)).astype(jnp.bfloat16)
    out[:, half:] = total(own_ref[0], near_ref[...])
    out[:, :half] = total(row_ref[...], corner_ref[...])


def placed(kernel, number, late, outs, pieces, counts, whole):
    frames, rows, columns, features = whole.shape
    lanes = features // 2
    outs = () if outs is None else outs
    shape = lambda p, n: ((n,) + p.shape[1:]) if p.ndim == 5 else p.shape
    full = lane_block((frames // 2, rows, columns, 0), lanes, lambda late: (late[0], 0, 0))
    return called(
        kernel,
        late,
        (*pieces, *outs),
        [lane_block(shape(p, n), lanes) for p, n in zip(pieces, counts)]
        + [pl.BlockSpec(memory_space=pl.ANY)] * len(outs),
        [full] * number,
        [jax.ShapeDtypeStruct(whole.shape, whole.dtype)] * number,
        features // lanes,
        {1 + len(pieces) + i: i for i in range(len(outs))},
    )


def after(value, *earlier):
    return lax.optimization_barrier((value,) + earlier)[0]


def shards(queries, keys, values, out_grad):
    inputs = (queries, keys, values, out_grad)
    frames, rows, columns, features = queries.shape
    time = lax.axis_index("tm")
    late = [jnp.where(time % 2 == parity, 1, 0).astype(jnp.int32) for parity in (0, 1)]

    def cut(xs, parity, row_start):
        sizes = (frames // 2, rows // 2, columns, features)
        start = (late[parity] * (frames // 2), row_start, 0, 0)
        return jnp.stack([lax.dynamic_slice(x, start, sizes) for x in xs])

    def near_of(parity, *wait):
        return moved(after(cut((queries, out_grad), parity, rows // 2), *wait), parity, 0)

    def row_of(xs, parity, *wait):
        return moved(after(cut(xs, parity, 0), *wait), None, -1)

    def rows_of_both(parity, *wait):
        return [row_of((x,), parity, *wait) for x in (keys, values)]

    qg = (queries, out_grad)
    spot = [flag.reshape(1) for flag in late]
    near0 = near_of(0)
    row_qg0 = row_of(qg, 0)
    corner0 = moved(row_qg0, 0, 0)
    row_kv0 = rows_of_both(0, row_qg0)
    near1 = near_of(1, near0)
    got0 = (row_qg0, *row_kv0, near0, corner0)
    stats0 = family_stats(spot[0], inputs, got0)
    other0 = moved(stats0, 0, 0)
    row_qg1 = jnp.concatenate([row_of((x,), 1, *row_kv0) for x in qg])
    row_kv1 = rows_of_both(1, other0)
    corner1 = moved(after(row_qg1, other0, near1), 1, 0)
    kept0, row0, pair0, near_b0, corner_b0 = family_grads(
        spot[0], inputs, got0, stats0, other0, True
    )
    got1 = (row_qg1, *row_kv1, near1, after(corner1, corner_b0))
    stats1 = family_stats(spot[1], inputs, got1)
    other1 = moved(stats1, 1, 0)
    row0, pair0 = moved(after(row0, *row_kv1), None, 1), moved(pair0, None, 1)
    near_b0 = moved(near_b0, 0, 0)
    corner_b0 = moved(after(corner_b0, other1, near_b0, row0, pair0), 0, 1)
    kept1, *rows1, near_b1, corner_b1 = family_grads(
        spot[1], inputs, got1, stats1, other1, False
    )
    near_b1 = moved(near_b1, 1, 0)
    corner_b1 = moved(after(corner_b1, near_b0, corner_b0), 1, 1)
    row1, *pair1 = [moved(r, None, 1) for r in rows1]
    pair = placed(place_pair_kernel, 2, spot[0], None, (kept0, pair0), (3, 2), queries)
    total = placed(
        place_sum_kernel, 1, spot[0], None, (kept0, row0, near_b0, corner_b0), (1, 1, 1, 1), queries
    )
    pair = placed(place_pair_kernel, 2, spot[1], pair, (kept1, *pair1), (3, 1, 1), queries)
    total = placed(
        place_sum_kernel, 1, spot[1], total, (kept1, row1, near_b1, corner_b1), (1, 1, 1, 1), queries
    )
    return (total[0], pair[0], pair[1])


def solution(mesh):
    spec = P("tm", "rows", None, None)
    return jax.shard_map(
        shards,
        mesh=mesh,
        in_specs=(spec,) * 4,
        out_specs=(spec,) * 3,
        check_vma=False,
    )
```

```python
import math

import jax
import jax.numpy as jnp
from jax import lax
from jax.experimental import pallas as pl
from jax.experimental.pallas import tpu as pltpu
from jax.sharding import PartitionSpec as P

WW = 8
HEAD_DIM = 128
AXES = ("tm", "rows")
VMEM_BYTES = 40 * 1024 * 1024


def moved(value, parity, by_rows):
    times, rows = lax.axis_size("tm"), lax.axis_size("rows")
    pairs = []
    for t in range(times):
        step = 0 if parity is None else (1 if t % 2 == parity else -1)
        for r in range(rows):
            pairs.append((t * rows + r, ((t + step) % times) * rows + (r + by_rows) % rows))
    return lax.ppermute(value, AXES, pairs)


def middle(shape):
    column = lax.broadcasted_iota(jnp.int32, shape, 1)
    return (column >= WW // 2) & (column < WW + WW // 2)


def turned(tokens):
    return jnp.concatenate((tokens[:, WW:], tokens[:, :WW]), axis=1)


def split_windows(parts):
    first, second = parts[0], turned(parts[1])
    inside = middle(first.shape)
    flat = (first.shape[0] * first.shape[1], first.shape[2])
    inner = jnp.where(inside, first, second).reshape(flat)
    outer = jnp.where(inside, second, first).reshape(flat)
    return inner, outer


def join_windows(inner, outer, slots):
    shape = (slots, 2 * WW, inner.shape[1])
    inner = inner.astype(jnp.bfloat16).reshape(shape)
    outer = outer.astype(jnp.bfloat16).reshape(shape)
    inside = middle(shape)
    return jnp.where(inside, inner, outer), turned(jnp.where(inside, outer, inner))


def dot(a, b, dims):
    return lax.dot_general(a, b, (dims, ((), ())), preferred_element_type=jnp.float32)


def key_sum(value):
    return jnp.sum(value, axis=0, keepdims=True)


def products(query, key, value, grad):
    factor = 1.0 / math.sqrt(HEAD_DIM)
    scores = dot(key, query, ((1,), (1,))) * factor
    weight_grad = dot(value, grad, ((1,), (1,)))
    return scores, weight_grad


def partial_stats(query, key, value, grad):
    scores, weight_grad = products(query, key, value, grad)
    top = jnp.max(scores, axis=0, keepdims=True)
    powers = jnp.exp(scores - top)
    return top, key_sum(powers), key_sum(powers * weight_grad)


def partial_grads(windows, mine, other):
    factor = 1.0 / math.sqrt(HEAD_DIM)
    each = range(len(windows))
    made = [products(*w) for w in windows]
    tops, inverses, row_dots = [], [], []
    for a, b in zip(mine, other):
        top = jnp.maximum(a[0], b[0])
        scale_a, scale_b = jnp.exp(a[0] - top), jnp.exp(b[0] - top)
        inverse = 1.0 / (a[1] * scale_a + b[1] * scale_b)
        tops.append(top)
        inverses.append(inverse)
        row_dots.append((a[2] * scale_a + b[2] * scale_b) * inverse)
    weights = [jnp.exp(made[i][0] - tops[i]) * inverses[i] for i in each]
    weights_b = [w.astype(jnp.bfloat16) for w in weights]
    score_grads = [
        (weights[i] * ((made[i][1] - row_dots[i]) * factor)).astype(jnp.bfloat16) for i in each
    ]
    value_out = [dot(weights_b[i], windows[i][3], ((1,), (0,))) for i in each]
    key_out = [dot(score_grads[i], windows[i][0], ((1,), (0,))) for i in each]
    query_out = [dot(score_grads[i], windows[i][1], ((0,), (0,))) for i in each]
    return list(zip(query_out, key_out, value_out))


def window_tokens(refs, head):
    q_ref, k_ref, v_ref, g_ref, qg_ref, key_row_ref, value_row_ref, near_ref, corner_ref = refs
    frames, rows, columns, _ = q_ref.shape
    lanes = pl.ds(head * HEAD_DIM, HEAD_DIM)
    flat = lambda p: p.reshape(frames * rows, columns, HEAD_DIM)
    at = lambda ref, *index: flat(ref[(*index, slice(None), slice(None), slice(None), lanes)])
    query = split_windows([at(q_ref), at(qg_ref, 0)])
    grad = split_windows([at(g_ref), at(qg_ref, 1)])
    key = split_windows([at(k_ref), at(key_row_ref, 0)])
    value = split_windows([at(v_ref), at(value_row_ref, 0)])
    far_query = split_windows([at(near_ref, 0), at(corner_ref, 0)])
    far_grad = split_windows([at(near_ref, 1), at(corner_ref, 1)])
    both = lambda own, far: jnp.concatenate((own, far), axis=0)
    return [
        (both(query[w], far_query[w]), key[w], value[w], both(grad[w], far_grad[w])) for w in (0, 1)
    ]


def stats_kernel(late_ref, *refs):
    out = refs[9]
    for head in range(out.shape[0]):
        found = []
        for window in window_tokens(refs[:9], head):
            found.extend(partial_stats(*window))
        blank = jnp.zeros_like(found[0])
        out[head] = jnp.concatenate(found + [blank] * (out.shape[1] - len(found)), axis=0)


def grads_kernel(late_ref, *refs):
    mine_ref, other_ref, kept_out = refs[9:12]
    near_out, corner_out = refs[-2:]
    row_outs = refs[12:15] if len(refs) == 17 else [refs[12], refs[13].at[0], refs[13].at[1]]
    _, frames, rows, columns, width = kept_out.shape
    shape = (frames, rows, columns, HEAD_DIM)
    for head in range(width // HEAD_DIM):
        lanes = pl.ds(head * HEAD_DIM, HEAD_DIM)
        windows = window_tokens(refs[:9], head)
        half = windows[0][1].shape[0]
        stat = lambda ref, w: [ref[head, pl.ds(3 * w + i, 1)] for i in range(3)]
        swapped = lambda o: jnp.concatenate((o[:, half:], o[:, :half]), axis=1)
        mine = [stat(mine_ref, w) for w in (0, 1)]
        other = [[swapped(o) for o in stat(other_ref, w)] for w in (0, 1)]
        grads = partial_grads(windows, mine, other)
        kept = [[g[0][:half] for g in grads], [g[1] for g in grads], [g[2] for g in grads]]
        for index, windows in enumerate(kept):
            tokens = [p.reshape(shape) for p in join_windows(*windows, frames * rows)]
            kept_out[index, :, :, :, lanes] = tokens[0]
            row_outs[index][:, :, :, lanes] = tokens[1]
        tokens = [p.reshape(shape) for p in join_windows(*[g[0][half:] for g in grads], frames * rows)]
        near_out[:, :, :, lanes] = tokens[0]
        corner_out[:, :, :, lanes] = tokens[1]


def lane_block(shape, lanes, place=None):
    index = lambda h, late: ((0,) * (len(shape) - 1) if place is None else place(late)) + (h,)
    return pl.BlockSpec(tuple(shape[:-1]) + (lanes,), index)


def heads_per_step(heads):
    return next(n for n in range(14, 0, -1) if heads % n == 0)


def small():
    return pl.CostEstimate(flops=1, bytes_accessed=1, transcendentals=0)


def called(kernel, late, operands, in_specs, out_specs, out_shape, steps, aliases=None):
    return pl.pallas_call(
        kernel,
        grid_spec=pltpu.PrefetchScalarGridSpec(
            num_scalar_prefetch=1, grid=(steps,), in_specs=in_specs, out_specs=out_specs
        ),
        out_shape=out_shape,
        input_output_aliases=aliases or {},
        compiler_params=pltpu.CompilerParams(vmem_limit_bytes=VMEM_BYTES),
        cost_estimate=small(),
    )(late, *operands)


def window_specs(inputs, received, lanes):
    frames, rows, columns, _ = inputs[0].shape
    own = lane_block((frames // 2, rows // 2, columns, 0), lanes, lambda late: (late[0], 1, 0))
    return [own] * 4 + [lane_block(r.shape, lanes) for r in received]


def stats_block(heads, length):
    return pl.BlockSpec((heads, 8, length), lambda h, late: (h, 0, 0))


def family_stats(late, inputs, received):
    frames, rows, _, features = inputs[0].shape
    heads, length = features // HEAD_DIM, frames * rows * WW
    step = heads_per_step(heads)
    return called(
        stats_kernel,
        late,
        (*inputs, *received),
        window_specs(inputs, received, step * HEAD_DIM),
        stats_block(step, length),
        jax.ShapeDtypeStruct((heads, 8, length), jnp.float32),
        heads // step,
    )


def family_grads(late, inputs, received, mine, other, joined):
    frames, rows, columns, features = inputs[0].shape
    heads, length = features // HEAD_DIM, frames * rows * WW
    step = heads_per_step(heads)
    sent = jax.ShapeDtypeStruct((frames // 2, rows // 2, columns, features), jnp.bfloat16)
    kept = jax.ShapeDtypeStruct((3,) + sent.shape, jnp.bfloat16)
    two = jax.ShapeDtypeStruct((2,) + sent.shape, jnp.bfloat16)
    shapes = [kept, sent] + ([two] if joined else [sent, sent]) + [sent, sent]
    return called(
        grads_kernel,
        late,
        (*inputs, *received, mine, other),
        window_specs(inputs, received, step * HEAD_DIM) + [stats_block(step, length)] * 2,
        [lane_block(s.shape, step * HEAD_DIM) for s in shapes],
        shapes,
        heads // step,
    )


def place_pair_kernel(late_ref, *refs):
    own_ref, outs = refs[0], refs[-2:]
    row_refs = refs[1:3] if refs[1].ndim == 4 else [refs[1].at[0], refs[1].at[1]]
    for index, out in enumerate(outs):
        half = out.shape[1] // 2
        out[:, half:] = own_ref[1 + index]
        out[:, :half] = row_refs[index][...]


def place_sum_kernel(late_ref, *refs):
    own_ref, row_ref, near_ref, corner_ref = refs[:4]
    out = refs[-1]
    half = out.shape[1] // 2
    row_ref, near_ref = [r if r.ndim == 4 else r.at[0] for r in (row_ref, near_ref)]
    total = lambda a, b: (a.astype(jnp.float32) + b.astype(jnp.float32)).astype(jnp.bfloat16)
    out[:, half:] = total(own_ref[0], near_ref[...])
    out[:, :half] = total(row_ref[...], corner_ref[...])


def placed(kernel, number, late, outs, pieces, counts, whole):
    frames, rows, columns, features = whole.shape
    lanes = features // 2
    outs = () if outs is None else outs
    shape = lambda p, n: ((n,) + p.shape[1:]) if p.ndim == 5 else p.shape
    full = lane_block((frames // 2, rows, columns, 0), lanes, lambda late: (late[0], 0, 0))
    return called(
        kernel,
        late,
        (*pieces, *outs),
        [lane_block(shape(p, n), lanes) for p, n in zip(pieces, counts)]
        + [pl.BlockSpec(memory_space=pl.ANY)] * len(outs),
        [full] * number,
        [jax.ShapeDtypeStruct(whole.shape, whole.dtype)] * number,
        features // lanes,
        {1 + len(pieces) + i: i for i in range(len(outs))},
    )


def after(value, *earlier):
    return lax.optimization_barrier((value,) + earlier)[0]


def shards(queries, keys, values, out_grad):
    inputs = (queries, keys, values, out_grad)
    frames, rows, columns, features = queries.shape
    time = lax.axis_index("tm")
    late = [jnp.where(time % 2 == parity, 1, 0).astype(jnp.int32) for parity in (0, 1)]

    def cut(xs, parity, row_start):
        sizes = (frames // 2, rows // 2, columns, features)
        start = (late[parity] * (frames // 2), row_start, 0, 0)
        return jnp.stack([lax.dynamic_slice(x, start, sizes) for x in xs])

    def near_of(parity, *wait):
        return moved(after(cut((queries, out_grad), parity, rows // 2), *wait), parity, 0)

    def row_of(xs, parity, *wait):
        return moved(after(cut(xs, parity, 0), *wait), None, -1)

    def rows_of_both(parity, *wait):
        return [row_of((x,), parity, *wait) for x in (keys, values)]

    qg = (queries, out_grad)
    spot = [flag.reshape(1) for flag in late]
    near0 = near_of(0)
    row_qg0 = row_of(qg, 0)
    corner0 = moved(row_qg0, 0, 0)
    row_kv0 = rows_of_both(0, row_qg0)
    near1 = near_of(1, near0)
    got0 = (row_qg0, *row_kv0, near0, corner0)
    stats0 = family_stats(spot[0], inputs, got0)
    other0 = moved(stats0, 0, 0)
    row_qg1 = jnp.concatenate([row_of((x,), 1, *row_kv0) for x in qg])
    row_kv1 = rows_of_both(1, other0)
    corner1 = moved(after(row_qg1, stats0, near1), 1, 0)
    kept0, row0, pair0, near_b0, corner_b0 = family_grads(
        spot[0], inputs, got0, stats0, other0, True
    )
    got1 = (row_qg1, *row_kv1, near1, after(corner1, corner_b0))
    stats1 = family_stats(spot[1], inputs, got1)
    other1 = moved(stats1, 1, 0)
    row0, pair0 = moved(after(row0, *row_kv1), None, 1), moved(pair0, None, 1)
    near_b0 = moved(near_b0, 0, 0)
    corner_b0 = moved(after(corner_b0, other1, near_b0, row0, pair0), 0, 1)
    kept1, *rows1, near_b1, corner_b1 = family_grads(
        spot[1], inputs, got1, stats1, other1, False
    )
    near_b1 = moved(near_b1, 1, 0)
    corner_b1 = moved(after(corner_b1, near_b0, corner_b0), 1, 1)
    row1, *pair1 = [moved(r, None, 1) for r in rows1]
    pair = placed(place_pair_kernel, 2, spot[0], None, (kept0, pair0), (3, 2), queries)
    total = placed(
        place_sum_kernel, 1, spot[0], None, (kept0, row0, near_b0, corner_b0), (1, 1, 1, 1), queries
    )
    pair = placed(place_pair_kernel, 2, spot[1], pair, (kept1, *pair1), (3, 1, 1), queries)
    total = placed(
        place_sum_kernel, 1, spot[1], total, (kept1, row1, near_b1, corner_b1), (1, 1, 1, 1), queries
    )
    return (total[0], pair[0], pair[1])


def solution(mesh):
    spec = P("tm", "rows", None, None)
    return jax.shard_map(
        shards,
        mesh=mesh,
        in_specs=(spec,) * 4,
        out_specs=(spec,) * 3,
        check_vma=False,
    )
```
